32 devices in a mesh: grp: 2 (over y), dp: 4 (over z), tensor: 4 (over x, core).
Axes of the slice: x: 2, y: 2, z: 4, core: 2. Of those that a mesh axis runs over, the one named last changes fastest.
Arguments:
- resid: bfloat16 [16, 2, 8192], P(('grp', 'dp'), None, 'tensor'), parts along dimension 0, may hold values from -6 to 6
- queries: bfloat16 [16, 2, 64, 128], P(('grp', 'dp'), None, 'tensor'), parts along dimension 0, may hold values from -12.5 to 12.5
- new_kv: bfloat16 [16, 3, 4, 2, 128], P(('grp', 'dp'), None, 'tensor'), parts along dimension 0, may hold values from -12.5 to 12.5
- tail_fill: int32 [16, 2], P(('grp', 'dp')), parts along dimension 0, may hold values from 1 to 16
- page_ids: int32 [16, 2, 4, 32], P(('grp', 'dp'), None, 'tensor'), parts along dimension 0, may hold values from 0 to 2559, as said below
- kv_pool: bfloat16 [5120, 2, 16, 128], P(('grp', 'dp', 'tensor')), parts along dimension 0, may hold values from -6 to 6
- norm_gain: float32 [8192], replicated, may hold values from 0.1 to 1.9
- gate_weight: bfloat16 [8192, 26624], P(None, ('dp', 'tensor')), may hold values from -0.0625 to 0.0625
- up_weight: bfloat16 [8192, 26624], P(None, ('dp', 'tensor')), may hold values from -0.0625 to 0.0625
- down_weight: bfloat16 [26624, 8192], P(('dp', 'tensor')), may hold values from -0.0390625 to 0.0390625
Outputs:
- attended: bfloat16 [16, 2, 8192], P(('grp', 'dp'), None, 'tensor'), parts along dimension 0
- ffn_out: bfloat16 [32, 8192], P(('grp', 'dp', 'tensor')), parts along dimension 0
The draws below stay inside these ranges and needn't reach their ends.
There are 2 independent parts, one for each index of `grp`. The reference program is written for one: setup_inputs(seed, part) draws one part's arguments, and reference() takes and returns one part's arrays. A program takes and returns all parts, laid end to end along the dimension named above; an argument that names none is the same for every part. Nothing has to cross between parts.
Inputs may be any that keep to these rules, and one draw needn't show every extreme that they name: `page_ids`: for one dp index i and KV head g, the ids of rows i * 2 to (i + 1) * 2 - 1, all steps, head g are distinct; at most 16 of them lie in any one block of pool slots k * 160 to (k + 1) * 160 - 1, and in every draw some block holds exactly 16 of them for every such (i, g).
All inputs are finite; a program needn't handle non-finite values.
Results may differ from the reference program's by a relative error of at most 0.0081.
Values may be sent and summed in bfloat16 or wider, within the bound.
A program may use at most 192 MiB of HBM per device.

```python
import math
import jax
import jax.numpy as jnp
from jax import lax

HEADS = 64
KVH = 4
HD = 128
FF = 26624
PAGE = 16
SEL = 32
STEPS = 2
SLOTS_DEV = 160
ROWS_DEV = 2
D = 8192
ROWS = 8
POOL = 2560
CAP = 16
N_DP = 4
N_TENSOR = 4


def draw_queries(key, part):
    key = jax.random.fold_in(key, 21)
    shape_all = (ROWS, STEPS, HEADS, HD)
    values = 2.0 * jax.random.truncated_normal(key, -3.0, 3.0, shape_all, jnp.float32)
    return values.astype(jnp.bfloat16)


def draw_new_kv(key, part):
    key = jax.random.fold_in(key, 33)
    key_keys, key_values = jax.random.split(key)
    shape_half = (ROWS, STEPS + 1, KVH, HD)
    fresh_keys = 1.5 * jax.random.truncated_normal(key_keys, -3.0, 3.0, shape_half, jnp.float32)
    fresh_values = jax.random.truncated_normal(key_values, -3.0, 3.0, shape_half, jnp.float32)
    return jnp.stack([fresh_keys, fresh_values], axis=3).astype(jnp.bfloat16)


def draw_page_ids(key, part):
    key = jax.random.fold_in(key, 47)
    owner_total = N_DP * N_TENSOR
    request_total = ROWS_DEV * STEPS * SEL
    item_total = owner_total * CAP
    item_owner = jnp.arange(item_total, dtype=jnp.int32) // CAP
    item_copy = jnp.arange(item_total, dtype=jnp.int32) % CAP
    key_hot, key_rest = jax.random.split(key)
    hot_owner = jax.random.randint(key_hot, (), 0, owner_total)
    stride = SLOTS_DEV // CAP

    def one_device(device_key):
        key_order, key_base, key_shuffle = jax.random.split(device_key, 3)
        priority = jax.random.permutation(key_order, item_total).astype(jnp.int32)
        priority = jnp.where(item_owner == hot_owner, -1 - item_copy, priority)
        picked = jnp.argsort(priority, stable=True)[:request_total]
        owner_list = item_owner[picked]
        copy_list = item_copy[picked]
        base_slot = jax.random.randint(key_base, (owner_total,), 0, SLOTS_DEV)
        slot_list = (base_slot[owner_list] + copy_list * stride) % SLOTS_DEV
        slot_ids = owner_list * SLOTS_DEV + slot_list
        shuffle = jax.random.permutation(key_shuffle, request_total)
        return slot_ids[shuffle]
    device_keys = jax.random.split(key_rest, owner_total)
    every_list = jax.vmap(one_device)(device_keys)
    arranged = every_list.reshape(N_DP, N_TENSOR, ROWS_DEV, STEPS, SEL)
    arranged = jnp.transpose(arranged, (0, 2, 3, 1, 4))
    return arranged.reshape(ROWS, STEPS, KVH, SEL).astype(jnp.int32)


def set_ends(array, own_key, smallest, top_value):
    longest = array.shape.index(max(array.shape))
    spots = []
    for shift in (0, 1):
        where = [jax.random.randint(jax.random.fold_in(own_key, axis), (), 0, length) for axis, length in enumerate(array.shape)]
        where[longest] = (where[longest] + shift) % array.shape[longest]
        spots.append(tuple(where))
    return array.at[spots[0]].set(smallest).at[spots[1]].set(top_value)


def block_levels(key, dims, shards, smallest, high):
    level = 1.0
    for axis_at, shards_of in shards:
        draws = jax.random.uniform(jax.random.fold_in(jax.random.fold_in(key, 6), axis_at), (shards_of,), jnp.float32, smallest / len(shards), high / len(shards))
        level = level * jnp.repeat(jnp.exp(draws), dims[axis_at] // shards_of).reshape((-1,) + (1,) * (len(dims) - 1 - axis_at))
    return level


def bell_draw(own_key, extent, spread, bound, cuts=(), kind=jnp.bfloat16):
    entries = jax.random.normal(own_key, extent, jnp.float32) * spread
    if len(cuts) > 0:
        entries = block_levels(own_key, extent, cuts, -0.22, 0.18) * entries
    return jnp.clip(entries, min=-bound, max=bound).astype(kind)


def setup_inputs(seed: int = 0, part: int = 0) -> dict:
    keys = jax.random.split(jax.random.key(seed), 11)
    part_splits = jax.random.split(jax.random.fold_in(keys[10], part), 11)
    return {
        "resid": bell_draw(part_splits[0], (ROWS, STEPS, D), 1.0, 6.0, ((0, 4), (2, 4))),
        "queries": draw_queries(jax.random.fold_in(jax.random.fold_in(keys[10], part), 71), part),
        "new_kv": draw_new_kv(jax.random.fold_in(jax.random.fold_in(keys[10], part), 71), part),
        "tail_fill": set_ends(jax.random.randint(part_splits[3], (ROWS, STEPS), 1, PAGE + 1), jax.random.fold_in(part_splits[3], 1), 1, PAGE).astype(jnp.int32),
        "page_ids": draw_page_ids(jax.random.fold_in(jax.random.fold_in(keys[10], part), 71), part),
        "kv_pool": bell_draw(part_splits[5], (POOL, 2, PAGE, HD), 1.0, 6.0, ((0, 16),)),
        "norm_gain": jnp.clip(1.0 + 0.18 * jax.random.normal(keys[6], (D,), jnp.float32), 0.1, 1.9),
        "gate_weight": bell_draw(keys[7], (D, FF), D ** -0.5, 0.0625, ((1, 16),)),
        "up_weight": bell_draw(keys[8], (D, FF), D ** -0.5, 0.0625, ((1, 16),)),
        "down_weight": bell_draw(keys[9], (FF, D), FF ** -0.5, 0.0390625, ((0, 16),)),
    }


def attend_group(query_group, page_keys, page_values, fresh_keys, fresh_values, fill_count):
    score_scale = 1.0 / math.sqrt(query_group.shape[-1])
    query_float = query_group.astype(jnp.float32)
    page_scores = jnp.einsum('rshd,rskd->rshk', query_float, page_keys.astype(jnp.float32)) * score_scale
    fresh_scores = jnp.einsum('rshd,rjd->rshj', query_float, fresh_keys.astype(jnp.float32)) * score_scale
    key_index = jnp.arange(page_keys.shape[2], dtype=jnp.int32)
    page_valid = (key_index[None, None, :] >= PAGE) | (key_index[None, None, :] < fill_count[:, :, None])
    page_scores = jnp.where(page_valid[:, :, None, :], page_scores, -jnp.inf)
    fresh_index = jnp.arange(fresh_keys.shape[1], dtype=jnp.int32)
    step_index = jnp.arange(fill_count.shape[1], dtype=jnp.int32)
    fresh_valid = fresh_index[None, :] <= step_index[:, None] + 1
    fresh_scores = jnp.where(fresh_valid[None, :, None, :], fresh_scores, -jnp.inf)
    top_score = jnp.maximum(lax.optimization_barrier(jnp.max(page_scores, axis=-1)), lax.optimization_barrier(jnp.max(fresh_scores, axis=-1)))
    page_exp = jnp.exp(page_scores - top_score[..., None])
    fresh_exp = jnp.exp(fresh_scores - top_score[..., None])
    total = lax.optimization_barrier(jnp.sum(page_exp, axis=-1)) + lax.optimization_barrier(jnp.sum(fresh_exp, axis=-1))
    page_weights = (page_exp / total[..., None]).astype(jnp.bfloat16)
    fresh_weights = (fresh_exp / total[..., None]).astype(jnp.bfloat16)
    page_part = jnp.einsum('rshk,rskd->rshd', page_weights.astype(jnp.float32), page_values.astype(jnp.float32))
    fresh_part = jnp.einsum('rshj,rjd->rshd', fresh_weights.astype(jnp.float32), fresh_values.astype(jnp.float32))
    return page_part + fresh_part

def reference(resid, queries, new_kv, tail_fill, page_ids, kv_pool, norm_gain, gate_weight, up_weight, down_weight):
    row_count = resid.shape[0]
    step_count = resid.shape[1]
    group_size = HEADS // KVH
    grouped_queries = jnp.moveaxis(queries.reshape(row_count, step_count, KVH, group_size, HD), 2, 0)
    head_pages = jnp.moveaxis(page_ids, 2, 0)
    head_fresh = jnp.moveaxis(new_kv, 2, 0)

    def one_head(inputs):
        query_group, slot_list, fresh_pair = inputs
        fetched = kv_pool[slot_list]
        page_keys = fetched[:, :, :, 0].reshape(row_count, step_count, SEL * PAGE, HD)
        page_values = fetched[:, :, :, 1].reshape(row_count, step_count, SEL * PAGE, HD)
        return attend_group(query_group, page_keys, page_values, fresh_pair[:, :, 0], fresh_pair[:, :, 1], tail_fill)
    per_head = lax.map(one_head, (grouped_queries, head_pages, head_fresh))
    attn = jnp.moveaxis(per_head, 0, 2).reshape(row_count, step_count, HEADS * HD)
    attended = (resid.astype(jnp.float32) + attn).astype(jnp.bfloat16)
    flat_rows = attended.reshape(row_count * step_count, HEADS * HD).astype(jnp.float32)
    mean_square = lax.optimization_barrier(jnp.mean(flat_rows * flat_rows, axis=-1, keepdims=True))
    normed = (flat_rows * lax.rsqrt(mean_square + 1e-05) * norm_gain).astype(jnp.bfloat16)
    gate_act = jnp.dot(normed, gate_weight, preferred_element_type=jnp.float32)
    up_act = jnp.dot(normed, up_weight, preferred_element_type=jnp.float32)
    hidden = (jax.nn.silu(gate_act) * up_act).astype(jnp.bfloat16)
    ffn_out = jnp.dot(hidden, down_weight, preferred_element_type=jnp.float32).astype(jnp.bfloat16)
    return (attended, ffn_out)
```

```python
import functools
import math

import jax
import jax.numpy as jnp
from jax import lax
from jax.experimental import pallas as pl
from jax.experimental.pallas import tpu as pltpu
from jax.sharding import PartitionSpec as P

PAGE = 16
SEL = 32


def attend_group(query_group, page_keys, page_values, fresh_keys, fresh_values, fill_count):
    score_scale = 1.0 / math.sqrt(query_group.shape[-1])
    page_scores = (
        jnp.einsum("rshd,rskd->rshk", query_group, page_keys, preferred_element_type=jnp.float32)
        * score_scale
    )
    fresh_scores = (
        jnp.einsum("rshd,rjd->rshj", query_group, fresh_keys, preferred_element_type=jnp.float32)
        * score_scale
    )
    key_index = jnp.arange(page_keys.shape[2], dtype=jnp.int32)
    page_valid = (key_index[None, None, :] >= PAGE) | (
        key_index[None, None, :] < fill_count[:, :, None]
    )
    page_scores = jnp.where(page_valid[:, :, None, :], page_scores, -jnp.inf)
    fresh_index = jnp.arange(fresh_keys.shape[1], dtype=jnp.int32)
    step_index = jnp.arange(fill_count.shape[1], dtype=jnp.int32)
    fresh_valid = fresh_index[None, :] <= step_index[:, None] + 1
    fresh_scores = jnp.where(fresh_valid[None, :, None, :], fresh_scores, -jnp.inf)
    top_score = jnp.maximum(jnp.max(page_scores, axis=-1), jnp.max(fresh_scores, axis=-1))
    page_exp = jnp.exp(page_scores - top_score[..., None])
    fresh_exp = jnp.exp(fresh_scores - top_score[..., None])
    total = jnp.sum(page_exp, axis=-1) + jnp.sum(fresh_exp, axis=-1)
    page_weights = (page_exp / total[..., None]).astype(jnp.bfloat16)
    fresh_weights = (fresh_exp / total[..., None]).astype(jnp.bfloat16)
    page_part = jnp.einsum(
        "rshk,rskd->rshd", page_weights, page_values, preferred_element_type=jnp.float32
    )
    fresh_part = jnp.einsum(
        "rshj,rjd->rshd", fresh_weights, fresh_values, preferred_element_type=jnp.float32
    )
    return page_part + fresh_part


def shards(
    resid,
    queries,
    new_kv,
    tail_fill,
    page_ids,
    kv_pool,
    norm_gain,
    gate_weight,
    up_weight,
    down_weight,
):
    owner_total = lax.axis_size("dp") * lax.axis_size("tensor")
    pool_slots = kv_pool.shape[0]
    row_count = resid.shape[0]
    step_count = resid.shape[1]
    slot_list = page_ids.reshape(-1)
    request_total = slot_list.shape[0]
    capacity = max(2, (2 * request_total + owner_total - 1) // owner_total)
    owner_list = slot_list // pool_slots
    local_list = slot_list % pool_slots
    owner_onehot = (
        owner_list[:, None] == jnp.arange(owner_total, dtype=jnp.int32)[None, :]
    ).astype(jnp.int32)
    order_rank = jnp.sum(jnp.cumsum(owner_onehot, axis=0) * owner_onehot, axis=1) - 1
    position = owner_list * capacity + order_rank
    request_buffer = jnp.zeros((owner_total * capacity,), jnp.int32).at[position].set(local_list)
    request_buffer = request_buffer.reshape(owner_total, capacity)
    returned = lax.all_to_all(
        kv_pool[
            lax.all_to_all(
                request_buffer, ("dp", "tensor"), split_axis=0, concat_axis=0, tiled=True
            )
        ],
        ("dp", "tensor"),
        split_axis=0,
        concat_axis=0,
        tiled=True,
    )
    page_rows = returned.reshape((owner_total * capacity,) + kv_pool.shape[1:])[position]
    page_rows = page_rows.reshape(row_count, step_count, SEL, 2, PAGE, kv_pool.shape[-1])
    page_keys = page_rows[:, :, :, 0].reshape(row_count, step_count, SEL * PAGE, kv_pool.shape[-1])
    page_values = page_rows[:, :, :, 1].reshape(
        row_count, step_count, SEL * PAGE, kv_pool.shape[-1]
    )
    fresh_pair = new_kv[:, :, 0]
    attn = attend_group(
        queries, page_keys, page_values, fresh_pair[:, :, 0], fresh_pair[:, :, 1], tail_fill
    )
    attn = attn.reshape(row_count, step_count, resid.shape[2])
    attended = (resid.astype(jnp.float32) + attn).astype(jnp.bfloat16)
    full_rows = lax.all_gather(attended, "tensor", axis=2, tiled=True).astype(jnp.float32)
    mean_square = jnp.mean(full_rows * full_rows, axis=-1, keepdims=True)
    normed = (full_rows * lax.rsqrt(mean_square + 1e-05) * norm_gain).astype(jnp.bfloat16)
    block_rows = lax.all_gather(normed, "dp", axis=0, tiled=True)
    flat_rows = block_rows.reshape(-1, block_rows.shape[-1])
    gate_act = jnp.dot(flat_rows, gate_weight, preferred_element_type=jnp.float32)
    up_act = jnp.dot(flat_rows, up_weight, preferred_element_type=jnp.float32)
    hidden_rows = (jax.nn.silu(gate_act) * up_act).astype(jnp.bfloat16)
    hidden_all = hidden_rows.reshape(block_rows.shape[0], block_rows.shape[1], -1)
    hidden_flat = hidden_all.reshape(-1, hidden_all.shape[-1])
    summed = lax.psum_scatter(
        jnp.dot(hidden_flat, down_weight, preferred_element_type=jnp.float32),
        ("dp", "tensor"),
        scatter_dimension=0,
        tiled=True,
    )
    ffn_out = summed.astype(jnp.bfloat16)
    return (attended, ffn_out)


def fits_fused(mesh, resid, queries, page_ids, kv_pool, gate_weight):
    owners = mesh.shape["dp"] * mesh.shape["tensor"]
    rows = resid.shape[0] // (mesh.shape["grp"] * mesh.shape["dp"])
    steps = resid.shape[1]
    wide = gate_weight.shape[1] // owners
    return (
        owners == 16
        and rows * steps * mesh.shape["dp"] == owners
        and (queries.shape[2] // mesh.shape["tensor"]) % 8 == 0
        and rows * steps * (queries.shape[2] // mesh.shape["tensor"]) == 64
        and rows * steps * page_ids.shape[3] == 128
        and queries.shape[3] == 128
        and wide % 128 == 0
        and 4 * wide <= gate_weight.shape[0]
        and gate_weight.shape[0] % 1024 == 0
    )


def fused_kernel(
    dims,
    q_ref,
    meta_ref,
    fresh_k_ref,
    fresh_v_ref,
    resid_ref,
    gain_ref,
    pool_hbm,
    gate_hbm,
    up_hbm,
    down_hbm,
    att_ref,
    out_ref,
    ring,
    pool,
    meta_all,
    q_all,
    o_send,
    o_all,
    ml_send,
    ml_all,
    x_all,
    list_vmem,
    list_smem,
    code_ref,
    y_ref,
    x_ref,
    h_ref,
    part_ref,
    p_send,
    p_all,
    pool_sem,
    list_sem,
    ring_sem,
    send_sem,
    meta_sem,
    q_sem,
    o_sem,
    ml_sem,
    x_sem,
    p_sem,
):
    n_dp, n_tensor, slots, wide, depth, ring_slots, rows, steps, heads, sel = dims
    owners = n_dp * n_tensor
    dp = lax.axis_index("dp")
    tensor = lax.axis_index("tensor")
    me = dp * n_tensor + tensor
    chunks = wide // 128
    down_loads = depth // 1024
    loads = chunks + down_loads
    quer = rows * steps * heads
    pages = rows * steps * sel

    def gate_copies(load, slot):
        column = pl.multiple_of(load * 128, 128)
        return [
            pltpu.make_async_copy(
                source.at[:, pl.ds(column, 128)],
                ring.at[slot, :, pl.ds(128 * half, 128)],
                ring_sem.at[slot, half],
            )
            for half, source in ((0, gate_hbm), (1, up_hbm))
        ]

    def down_copies(load, slot):
        return [
            pltpu.make_async_copy(
                down_hbm.at[:, pl.ds(pl.multiple_of(load * 1024 + 256 * q, 256), 256)],
                ring.at[slot, pl.ds(q * wide, wide), :],
                ring_sem.at[slot, q],
            )
            for q in range(4)
        ]

    pool_copy = pltpu.make_async_copy(pool_hbm, pool, pool_sem)
    pool_copy.start()

    def peer_of(offset):
        peer = lax.rem(me + offset, owners)
        return peer, {"dp": peer // n_tensor, "tensor": peer % n_tensor}

    def remote(kind, source, target, sems, peer, device, index):
        return pltpu.make_async_remote_copy(
            src_ref=source,
            dst_ref=target,
            send_sem=send_sem.at[kind, peer],
            recv_sem=sems.at[index],
            device_id=device,
            device_id_type=pl.DeviceIdType.MESH,
        )

    barrier = pltpu.get_barrier_semaphore()

    def greet(offset, carry):
        _, device = peer_of(offset)
        pl.semaphore_signal(barrier, inc=1, device_id=device, device_id_type=pl.DeviceIdType.MESH)
        return carry

    lax.fori_loop(1, owners, greet, 0)

    def preload(load, carry):
        for copy in gate_copies(load, load):
            copy.start()
        return carry

    lax.fori_loop(0, min(chunks, ring_slots), preload, 0)
    for load in range(chunks, ring_slots):
        for copy in down_copies(load - chunks, load):
            copy.start()

    pl.semaphore_wait(barrier, owners - 1)

    def send_queries(offset, carry):
        peer, device = peer_of(offset)
        remote(0, meta_ref, meta_all.at[me], meta_sem, peer, device, me).start()
        remote(1, q_ref, q_all.at[me], q_sem, peer, device, me).start()
        return carry

    lax.fori_loop(1, owners, send_queries, 0)
    meta_all[me] = meta_ref[...]
    q_all[me] = q_ref[...]

    scale = 1.0 / math.sqrt(q_ref.shape[-1])
    fresh_scores = (
        lax.dot_general(
            q_ref[...],
            fresh_k_ref[...],
            (((1,), (1,)), ((), ())),
            preferred_element_type=jnp.float32,
        )
        * scale
    )
    qi = lax.broadcasted_iota(jnp.int32, fresh_scores.shape, 0)
    fi = lax.broadcasted_iota(jnp.int32, fresh_scores.shape, 1)
    fresh = steps + 1
    fresh_ok = (fi // fresh == qi // (steps * heads)) & (
        fi % fresh <= (qi // heads) % steps + 1
    )
    fresh_scores = jnp.where(fresh_ok, fresh_scores, -1e30)
    fresh_top = jnp.max(fresh_scores, axis=1, keepdims=True)
    fresh_exp = jnp.where(fresh_ok, jnp.exp(fresh_scores - fresh_top), 0.0)
    fresh_total = jnp.sum(fresh_exp, axis=1, keepdims=True)
    fresh_out = jnp.dot(
        fresh_exp.astype(jnp.bfloat16), fresh_v_ref[...], preferred_element_type=jnp.float32
    )

    def as_rows(first, second):
        lane = lax.broadcasted_iota(jnp.int32, (quer, 128), 1)
        both = jnp.where(lane == 0, first, jnp.where(lane == 1, second, 0.0))
        both = jnp.concatenate([both, jnp.zeros((128 - quer, 128), jnp.float32)], axis=0)
        return jnp.transpose(both)[0:8]

    fresh_rows = as_rows(fresh_top, fresh_total)

    def wait_meta(offset, carry):
        peer, device = peer_of(offset)
        remote(0, meta_ref, meta_all.at[peer], meta_sem, peer, device, peer).wait_recv()
        return carry

    lax.fori_loop(1, owners, wait_meta, 0)

    ids = meta_all[:, 0, :]
    extra = meta_all[:, 1, :]
    local = ids - me * slots
    inside = (local >= 0) & (local < slots)
    row_i = lax.broadcasted_iota(jnp.int32, (pages, pages), 0)
    col_i = lax.broadcasted_iota(jnp.int32, (pages, pages), 1)
    before = jnp.where(row_i < col_i, 1.0, 0.0).astype(jnp.bfloat16)
    rank = jnp.dot(
        jnp.where(inside, 1.0, 0.0).astype(jnp.bfloat16), before, preferred_element_type=jnp.float32
    )
    capacity = max(2, (2 * pages + owners - 1) // owners)
    lane = lax.broadcasted_iota(jnp.int32, ids.shape, 1)
    slot_list = jnp.zeros(ids.shape, jnp.float32)
    code_list = jnp.zeros(ids.shape, jnp.float32)
    local_float = local.astype(jnp.float32)
    extra_float = extra.astype(jnp.float32)
    for k in range(capacity):
        chosen = inside & (rank == float(k))
        slot_k = jnp.sum(jnp.where(chosen, local_float, 0.0), axis=1, keepdims=True)
        code_k = jnp.sum(jnp.where(chosen, extra_float, 0.0), axis=1, keepdims=True)
        slot_list = jnp.where(lane == k, slot_k, slot_list)
        code_list = jnp.where(lane == k, code_k, code_list)
    list_vmem[...] = slot_list.astype(jnp.int32)
    list_copy = pltpu.make_async_copy(list_vmem, list_smem, list_sem)
    list_copy.start()
    keys = capacity * PAGE
    spread_k = lax.broadcasted_iota(jnp.int32, (pages, keys), 0)
    spread_c = lax.broadcasted_iota(jnp.int32, (pages, keys), 1)
    spread = jnp.where(spread_c // PAGE == spread_k, 1.0, 0.0).astype(jnp.bfloat16)
    code_ref[...] = jnp.dot(
        code_list.astype(jnp.bfloat16), spread, preferred_element_type=jnp.float32
    )
    list_copy.wait()
    pool_copy.wait()

    def attend(other, ready):
        code = code_ref[pl.ds(other, 1), :].astype(jnp.int32)
        key_rows = []
        value_rows = []
        for k in range(capacity):
            slot = jnp.clip(list_smem[other, k], 0, slots - 1)
            key_rows.append(pool[slot, 0])
            value_rows.append(pool[slot, 1])
        page_keys = jnp.concatenate(key_rows, axis=0)
        page_values = jnp.concatenate(value_rows, axis=0)
        scores = (
            lax.dot_general(
                q_all[other],
                page_keys,
                (((1,), (1,)), ((), ())),
                preferred_element_type=jnp.float32,
            )
            * scale
        )
        qi = lax.broadcasted_iota(jnp.int32, scores.shape, 0)
        ki = lax.broadcasted_iota(jnp.int32, scores.shape, 1)
        valid = (qi // heads == code // 32) & (ki % PAGE < code % 32)
        scores = jnp.where(valid, scores, -1e30)
        top = jnp.max(scores, axis=1, keepdims=True)
        weights = jnp.where(valid, jnp.exp(scores - top), 0.0)
        total = jnp.sum(weights, axis=1, keepdims=True)
        mixed = jnp.dot(
            weights.astype(jnp.bfloat16), page_values, preferred_element_type=jnp.float32
        )
        o_send[other] = mixed.astype(jnp.bfloat16)
        ml_send[other] = as_rows(top, total)

    def attend_peer(offset, carry):
        peer, device = peer_of(offset)
        remote(1, q_ref, q_all.at[peer], q_sem, peer, device, peer).wait_recv()
        attend(peer, None)
        remote(2, o_send.at[peer], o_all.at[me], o_sem, peer, device, me).start()
        remote(3, ml_send.at[peer], ml_all.at[me], ml_sem, peer, device, me).start()
        return carry

    lax.fori_loop(1, owners, attend_peer, 0)
    attend(me, None)
    o_all[me] = o_send[me]
    ml_all[me] = ml_send[me]

    def wait_parts(offset, carry):
        peer, device = peer_of(offset)
        remote(2, o_send.at[peer], o_all.at[peer], o_sem, peer, device, peer).wait_recv()
        remote(3, ml_send.at[peer], ml_all.at[peer], ml_sem, peer, device, peer).wait_recv()
        return carry

    lax.fori_loop(1, owners, wait_parts, 0)

    tops = ml_all[:, 0, :]
    totals = ml_all[:, 1, :]
    top = jnp.maximum(jnp.max(tops, axis=0, keepdims=True), fresh_rows[0:1])
    shares = jnp.exp(tops - top)
    fresh_share = jnp.exp(fresh_rows[0:1] - top)
    total = jnp.sum(shares * totals, axis=0, keepdims=True) + fresh_share * fresh_rows[1:2]
    total = jnp.where(lane[0:1] < quer, total, 1.0)
    shares = shares / total
    fresh_share = fresh_share / total
    every = jnp.concatenate(
        [shares, fresh_share, jnp.zeros((128 - owners - 1, 128), jnp.float32)], axis=0
    )
    columns = jnp.transpose(every)
    attn = fresh_out * columns[0:quer, owners : owners + 1]
    for owner in range(owners):
        attn = attn + o_all[owner].astype(jnp.float32) * columns[0:quer, owner : owner + 1]
    attended = (resid_ref[...].astype(jnp.float32) + attn).astype(jnp.bfloat16)
    att_ref[...] = attended
    x_all[me] = attended

    def send_rows(offset, carry):
        peer, device = peer_of(offset)
        remote(4, x_all.at[me], x_all.at[me], x_sem, peer, device, me).start()
        return carry

    lax.fori_loop(1, owners, send_rows, 0)

    def wait_rows(offset, carry):
        peer, device = peer_of(offset)
        remote(4, x_all.at[peer], x_all.at[peer], x_sem, peer, device, peer).wait_recv()
        return carry

    lax.fori_loop(1, owners, wait_rows, 0)

    each = rows * steps
    tiles = depth // 128
    for line in range(n_dp):
        block = jnp.concatenate(
            [
                x_all[line * n_tensor + part].astype(jnp.float32).reshape(each, heads, 128)
                for part in range(n_tensor)
            ],
            axis=1,
        )
        squares = jnp.sum(jnp.sum(block * block, axis=1, keepdims=True), axis=2, keepdims=True)
        block = block * lax.rsqrt(squares / depth + 1e-05) * gain_ref[...][None]
        y_ref[line * each : (line + 1) * each] = block
    for tile in range(tiles):
        x_ref[:, tile * 128 : (tile + 1) * 128] = y_ref[:, tile, :].astype(jnp.bfloat16)

    def hidden_step(load, carry):
        slot = load
        for copy in gate_copies(load, slot):
            copy.wait()
        both = jnp.dot(x_ref[...], ring[slot], preferred_element_type=jnp.float32)
        gate_act = both[:, :128]
        value = gate_act / (1.0 + jnp.exp(-gate_act)) * both[:, 128:]
        h_ref[:, pl.ds(pl.multiple_of(load * 128, 128), 128)] = value.astype(jnp.bfloat16)

        @pl.when(load + ring_slots < loads)
        def _():
            for copy in down_copies(load + ring_slots - chunks, slot):
                copy.start()

        return carry

    lax.fori_loop(0, chunks, hidden_step, 0)

    pieces = 2
    per_piece = down_loads // pieces
    rows_piece = tiles // pieces

    def piece_copy(piece, source, target, peer, device, index):
        lines = pl.ds(piece * rows_piece, rows_piece)
        return pltpu.make_async_remote_copy(
            src_ref=p_send.at[source, lines],
            dst_ref=p_all.at[target, lines],
            send_sem=send_sem.at[5 + piece, peer],
            recv_sem=p_sem.at[piece, index],
            device_id=device,
            device_id_type=pl.DeviceIdType.MESH,
        )

    for piece in range(pieces):
        for step in range(per_piece):
            load = piece * per_piece + step
            slot = (chunks + load) % ring_slots
            for copy in down_copies(load, slot):
                copy.wait()
            for q in range(4):
                both = jnp.dot(
                    h_ref[...],
                    ring[slot, q * wide : (q + 1) * wide, :],
                    preferred_element_type=jnp.float32,
                )
                tile = load * 8 + 2 * q
                part_ref[:, tile, :] = both[:, :128]
                part_ref[:, tile + 1, :] = both[:, 128:]

        lines = slice(piece * rows_piece, (piece + 1) * rows_piece)
        for owner in range(owners):
            p_send[owner, lines] = part_ref[owner, lines].astype(jnp.bfloat16)

        def send_piece(offset, carry):
            peer, device = peer_of(offset)
            piece_copy(piece, peer, me, peer, device, me).start()
            return carry

        lax.fori_loop(1, owners, send_piece, 0)

    for piece in range(pieces):
        lines = slice(piece * rows_piece, (piece + 1) * rows_piece)

        def wait_piece(offset, carry):
            peer, device = peer_of(offset)
            piece_copy(piece, peer, peer, peer, device, peer).wait_recv()
            return carry

        lax.fori_loop(1, owners, wait_piece, 0)
        p_all[me, lines] = p_send[me, lines]
        summed = p_all[0, lines].astype(jnp.float32)
        for owner in range(1, owners):
            summed = summed + p_all[owner, lines].astype(jnp.float32)
        out_ref[lines] = summed.astype(jnp.bfloat16)

    def drain(offset, carry):
        peer, device = peer_of(offset)
        remote(0, meta_ref, meta_all.at[me], meta_sem, peer, device, me).wait_send()
        remote(1, q_ref, q_all.at[me], q_sem, peer, device, me).wait_send()
        remote(2, o_send.at[peer], o_all.at[me], o_sem, peer, device, me).wait_send()
        remote(3, ml_send.at[peer], ml_all.at[me], ml_sem, peer, device, me).wait_send()
        remote(4, x_all.at[me], x_all.at[me], x_sem, peer, device, me).wait_send()
        for piece in range(pieces):
            piece_copy(piece, peer, me, peer, device, me).wait_send()
        return carry

    lax.fori_loop(1, owners, drain, 0)


RING_SLOTS = 14


def fused_shards(
    resid,
    queries,
    new_kv,
    tail_fill,
    page_ids,
    kv_pool,
    norm_gain,
    gate_weight,
    up_weight,
    down_weight,
):
    n_dp = lax.axis_size("dp")
    n_tensor = lax.axis_size("tensor")
    owners = n_dp * n_tensor
    rows, steps, heads, head = queries.shape
    sel = page_ids.shape[-1]
    slots = kv_pool.shape[0]
    depth, wide = gate_weight.shape
    quer = rows * steps * heads
    tiles = depth // 128
    page_at = jnp.arange(sel, dtype=jnp.int32)
    held = jnp.where(page_at[None, None, :] == 0, tail_fill[:, :, None], PAGE)
    reader = jnp.arange(rows * steps, dtype=jnp.int32).reshape(rows, steps, 1)
    meta = jnp.stack([page_ids.reshape(-1), (held + 32 * reader).reshape(-1)])
    meta = jnp.pad(meta, ((0, 6), (0, 0)))
    fresh = new_kv[:, :, 0].reshape(rows * (steps + 1), 2, head)
    fresh = jnp.pad(fresh, ((0, 16 - fresh.shape[0]), (0, 0), (0, 0)))
    capacity = max(2, (2 * rows * steps * sel + owners - 1) // owners)
    dims = (n_dp, n_tensor, slots, wide, depth, RING_SLOTS, rows, steps, heads, sel)
    bf16, f32, i32 = jnp.bfloat16, jnp.float32, jnp.int32
    vmem = pl.BlockSpec(memory_space=pltpu.VMEM)
    hbm = pl.BlockSpec(memory_space=pl.ANY)
    dma = pltpu.SemaphoreType.DMA
    attended, ffn_out = pl.pallas_call(
        functools.partial(fused_kernel, dims),
        out_shape=(
            jax.ShapeDtypeStruct((quer, head), bf16),
            jax.ShapeDtypeStruct((tiles, 128), bf16),
        ),
        in_specs=[vmem] * 6 + [hbm] * 4,
        out_specs=(vmem, vmem),
        scratch_shapes=[
            pltpu.VMEM((RING_SLOTS, depth, 256), bf16),
            pltpu.VMEM(kv_pool.shape, bf16),
            pltpu.VMEM((owners, 8, 128), i32),
            pltpu.VMEM((owners, quer, head), bf16),
            pltpu.VMEM((owners, quer, head), bf16),
            pltpu.VMEM((owners, quer, head), bf16),
            pltpu.VMEM((owners, 8, 128), f32),
            pltpu.VMEM((owners, 8, 128), f32),
            pltpu.VMEM((owners, quer, head), bf16),
            pltpu.VMEM((owners, 128), i32),
            pltpu.SMEM((owners, 128), i32),
            pltpu.VMEM((owners, capacity * PAGE), f32),
            pltpu.VMEM((owners, tiles, 128), f32),
            pltpu.VMEM((owners, depth), bf16),
            pltpu.VMEM((owners, wide), bf16),
            pltpu.VMEM((owners, tiles, 128), f32),
            pltpu.VMEM((owners, tiles, 128), bf16),
            pltpu.VMEM((owners, tiles, 128), bf16),
            dma(()),
            dma(()),
            dma((RING_SLOTS, 4)),
            dma((7, owners)),
            dma((owners,)),
            dma((owners,)),
            dma((owners,)),
            dma((owners,)),
            dma((owners,)),
            dma((2, owners)),
        ],
        compiler_params=pltpu.CompilerParams(
            collective_id=0, has_side_effects=True, vmem_limit_bytes=VMEM_LIMIT
        ),
        name="attend_ffn",
    )(
        queries.reshape(quer, head),
        meta,
        fresh[:, 0],
        fresh[:, 1],
        resid.reshape(quer, head),
        norm_gain.reshape(tiles, 128),
        kv_pool,
        gate_weight,
        up_weight,
        down_weight,
    )
    return attended.reshape(resid.shape), ffn_out.reshape(1, depth)


VMEM_LIMIT = 65 * 1000 * 1000


def solution(mesh):
    in_specs = (
        P(("grp", "dp"), None, "tensor"),
        P(("grp", "dp"), None, "tensor", None),
        P(("grp", "dp"), None, "tensor", None, None),
        P(("grp", "dp"), None),
        P(("grp", "dp"), None, "tensor", None),
        P(("grp", "dp", "tensor"), None, None, None),
        P(),
        P(None, ("dp", "tensor")),
        P(None, ("dp", "tensor")),
        P(("dp", "tensor"), None),
    )
    out_specs = (P(("grp", "dp"), None, "tensor"), P(("grp", "dp", "tensor"), None))

    def whole(*arrays):
        fused = fits_fused(mesh, arrays[0], arrays[1], arrays[4], arrays[5], arrays[7])
        return jax.shard_map(
            fused_shards if fused else shards,
            mesh=mesh,
            in_specs=in_specs,
            out_specs=out_specs,
            check_vma=False,
        )(*arrays)

    return whole
```

```python
import functools
import math

import jax
import jax.numpy as jnp
from jax import lax
from jax.experimental import pallas as pl
from jax.experimental.pallas import tpu as pltpu
from jax.sharding import PartitionSpec as P

PAGE = 16
SEL = 32


def attend_group(query_group, page_keys, page_values, fresh_keys, fresh_values, fill_count):
    score_scale = 1.0 / math.sqrt(query_group.shape[-1])
    page_scores = (
        jnp.einsum("rshd,rskd->rshk", query_group, page_keys, preferred_element_type=jnp.float32)
        * score_scale
    )
    fresh_scores = (
        jnp.einsum("rshd,rjd->rshj", query_group, fresh_keys, preferred_element_type=jnp.float32)
        * score_scale
    )
    key_index = jnp.arange(page_keys.shape[2], dtype=jnp.int32)
    page_valid = (key_index[None, None, :] >= PAGE) | (
        key_index[None, None, :] < fill_count[:, :, None]
    )
    page_scores = jnp.where(page_valid[:, :, None, :], page_scores, -jnp.inf)
    fresh_index = jnp.arange(fresh_keys.shape[1], dtype=jnp.int32)
    step_index = jnp.arange(fill_count.shape[1], dtype=jnp.int32)
    fresh_valid = fresh_index[None, :] <= step_index[:, None] + 1
    fresh_scores = jnp.where(fresh_valid[None, :, None, :], fresh_scores, -jnp.inf)
    top_score = jnp.maximum(jnp.max(page_scores, axis=-1), jnp.max(fresh_scores, axis=-1))
    page_exp = jnp.exp(page_scores - top_score[..., None])
    fresh_exp = jnp.exp(fresh_scores - top_score[..., None])
    total = jnp.sum(page_exp, axis=-1) + jnp.sum(fresh_exp, axis=-1)
    page_weights = (page_exp / total[..., None]).astype(jnp.bfloat16)
    fresh_weights = (fresh_exp / total[..., None]).astype(jnp.bfloat16)
    page_part = jnp.einsum(
        "rshk,rskd->rshd", page_weights, page_values, preferred_element_type=jnp.float32
    )
    fresh_part = jnp.einsum(
        "rshj,rjd->rshd", fresh_weights, fresh_values, preferred_element_type=jnp.float32
    )
    return page_part + fresh_part


def shards(
    resid,
    queries,
    new_kv,
    tail_fill,
    page_ids,
    kv_pool,
    norm_gain,
    gate_weight,
    up_weight,
    down_weight,
):
    owner_total = lax.axis_size("dp") * lax.axis_size("tensor")
    pool_slots = kv_pool.shape[0]
    row_count = resid.shape[0]
    step_count = resid.shape[1]
    slot_list = page_ids.reshape(-1)
    request_total = slot_list.shape[0]
    capacity = max(2, (2 * request_total + owner_total - 1) // owner_total)
    owner_list = slot_list // pool_slots
    local_list = slot_list % pool_slots
    owner_onehot = (
        owner_list[:, None] == jnp.arange(owner_total, dtype=jnp.int32)[None, :]
    ).astype(jnp.int32)
    order_rank = jnp.sum(jnp.cumsum(owner_onehot, axis=0) * owner_onehot, axis=1) - 1
    position = owner_list * capacity + order_rank
    request_buffer = jnp.zeros((owner_total * capacity,), jnp.int32).at[position].set(local_list)
    request_buffer = request_buffer.reshape(owner_total, capacity)
    returned = lax.all_to_all(
        kv_pool[
            lax.all_to_all(
                request_buffer, ("dp", "tensor"), split_axis=0, concat_axis=0, tiled=True
            )
        ],
        ("dp", "tensor"),
        split_axis=0,
        concat_axis=0,
        tiled=True,
    )
    page_rows = returned.reshape((owner_total * capacity,) + kv_pool.shape[1:])[position]
    page_rows = page_rows.reshape(row_count, step_count, SEL, 2, PAGE, kv_pool.shape[-1])
    page_keys = page_rows[:, :, :, 0].reshape(row_count, step_count, SEL * PAGE, kv_pool.shape[-1])
    page_values = page_rows[:, :, :, 1].reshape(
        row_count, step_count, SEL * PAGE, kv_pool.shape[-1]
    )
    fresh_pair = new_kv[:, :, 0]
    attn = attend_group(
        queries, page_keys, page_values, fresh_pair[:, :, 0], fresh_pair[:, :, 1], tail_fill
    )
    attn = attn.reshape(row_count, step_count, resid.shape[2])
    attended = (resid.astype(jnp.float32) + attn).astype(jnp.bfloat16)
    full_rows = lax.all_gather(attended, "tensor", axis=2, tiled=True).astype(jnp.float32)
    mean_square = jnp.mean(full_rows * full_rows, axis=-1, keepdims=True)
    normed = (full_rows * lax.rsqrt(mean_square + 1e-05) * norm_gain).astype(jnp.bfloat16)
    block_rows = lax.all_gather(normed, "dp", axis=0, tiled=True)
    flat_rows = block_rows.reshape(-1, block_rows.shape[-1])
    gate_act = jnp.dot(flat_rows, gate_weight, preferred_element_type=jnp.float32)
    up_act = jnp.dot(flat_rows, up_weight, preferred_element_type=jnp.float32)
    hidden_rows = (jax.nn.silu(gate_act) * up_act).astype(jnp.bfloat16)
    hidden_all = hidden_rows.reshape(block_rows.shape[0], block_rows.shape[1], -1)
    hidden_flat = hidden_all.reshape(-1, hidden_all.shape[-1])
    summed = lax.psum_scatter(
        jnp.dot(hidden_flat, down_weight, preferred_element_type=jnp.float32),
        ("dp", "tensor"),
        scatter_dimension=0,
        tiled=True,
    )
    ffn_out = summed.astype(jnp.bfloat16)
    return (attended, ffn_out)


def fits_fused(mesh, resid, queries, page_ids, kv_pool, gate_weight):
    owners = mesh.shape["dp"] * mesh.shape["tensor"]
    rows = resid.shape[0] // (mesh.shape["grp"] * mesh.shape["dp"])
    steps = resid.shape[1]
    wide = gate_weight.shape[1] // owners
    return (
        owners == 16
        and mesh.shape["tensor"] == 4
        and rows * steps * mesh.shape["dp"] == owners
        and (queries.shape[2] // mesh.shape["tensor"]) % 8 == 0
        and rows * steps * (queries.shape[2] // mesh.shape["tensor"]) == 64
        and rows * steps * page_ids.shape[3] == 128
        and queries.shape[3] == 128
        and wide % 128 == 0
        and 4 * wide <= gate_weight.shape[0]
        and gate_weight.shape[0] % 1024 == 0
    )


def fused_kernel(
    dims,
    q_ref,
    ids_ref,
    fill_ref,
    new_ref,
    resid_ref,
    gain_ref,
    pool_hbm,
    gate_hbm,
    up_hbm,
    down_hbm,
    att_ref,
    out_ref,
    ring,
    pool,
    meta_all,
    q_all,
    o_send,
    o_all,
    ml_send,
    ml_all,
    x_all,
    list_vmem,
    list_smem,
    code_ref,
    y_ref,
    x_ref,
    h_ref,
    part_ref,
    core_send,
    core_got,
    x_send,
    x_got,
    z_send,
    z_got,
    pool_sem,
    list_sem,
    ring_sem,
    send_sem,
    meta_sem,
    q_sem,
    o_sem,
    ml_sem,
    x_sem,
    p_send_sem,
    p_sem,
):
    n_dp, n_tensor, slots, wide, depth, ring_slots, rows, steps, heads, sel = dims
    owners = n_dp * n_tensor
    dp = lax.axis_index("dp")
    tensor = lax.axis_index("tensor")
    me = dp * n_tensor + tensor
    chunks = wide // 128
    down_loads = depth // 1024
    loads = chunks + down_loads
    quer = rows * steps * heads
    pages = rows * steps * sel

    def gate_copies(load, slot):
        column = pl.multiple_of(load * 128, 128)
        return [
            pltpu.make_async_copy(
                source.at[:, pl.ds(column, 128)],
                ring.at[slot, :, pl.ds(128 * half, 128)],
                ring_sem.at[slot, half],
            )
            for half, source in ((0, gate_hbm), (1, up_hbm))
        ]

    def down_copies(load, slot):
        return [
            pltpu.make_async_copy(
                down_hbm.at[:, pl.ds(pl.multiple_of(load * 1024 + 256 * q, 256), 256)],
                ring.at[slot, pl.ds(q * wide, wide), :],
                ring_sem.at[slot, q],
            )
            for q in range(4)
        ]

    pool_copy = pltpu.make_async_copy(pool_hbm, pool, pool_sem)
    pool_copy.start()

    def peer_of(offset):
        peer = lax.rem(me + offset, owners)
        return peer, {"dp": peer // n_tensor, "tensor": peer % n_tensor}

    def remote(kind, source, target, sems, peer, device, index):
        return pltpu.make_async_remote_copy(
            src_ref=source,
            dst_ref=target,
            send_sem=send_sem.at[kind, peer],
            recv_sem=sems.at[index],
            device_id=device,
            device_id_type=pl.DeviceIdType.MESH,
        )

    barrier = pltpu.get_barrier_semaphore()

    def greet(offset, carry):
        _, device = peer_of(offset)
        pl.semaphore_signal(barrier, inc=1, device_id=device, device_id_type=pl.DeviceIdType.MESH)
        return carry

    lax.fori_loop(1, owners, greet, 0)

    def preload(load, carry):
        for copy in gate_copies(load, load):
            copy.start()
        return carry

    lax.fori_loop(0, min(chunks, ring_slots), preload, 0)
    for load in range(chunks, ring_slots):
        for copy in down_copies(load - chunks, load):
            copy.start()

    pl.semaphore_wait(barrier, owners - 1)

    meta_all[me] = jnp.zeros((8, 128), jnp.int32)
    page_lane = lax.broadcasted_iota(jnp.int32, (1, 128), 1)
    held = PAGE + 32 * (page_lane // sel)
    for row in range(rows):
        for step in range(steps):
            at = (row * steps + step) * sel
            meta_all[me, 0:1, at : at + sel] = ids_ref[row, step]
            held = jnp.where(page_lane == at, fill_ref[row, step] + 32 * (at // sel), held)
    meta_all[me, 1:2, :] = held
    q_all[me] = q_ref[...]

    core_peer = tensor + 1 - 2 * lax.rem(tensor, 2)
    x_peer = lax.rem(tensor + 2, 4)

    def forward(kind, buffer, sems, block, device, index):
        return pltpu.make_async_remote_copy(
            src_ref=buffer.at[block],
            dst_ref=buffer.at[block],
            send_sem=send_sem.at[kind, index],
            recv_sem=sems.at[block],
            device_id=device,
            device_id_type=pl.DeviceIdType.MESH,
        )

    to_core = {"dp": dp, "tensor": core_peer}
    to_x = {"dp": dp, "tensor": x_peer}

    def spread_out(sets):
        def line_of(offset):
            line = lax.rem(dp + offset, n_dp)
            return line, line * n_tensor

        for offset in range(1, n_dp):
            line, _ = line_of(offset)
            for kind, buffer, sems in sets:
                forward(
                    kind, buffer, sems, me, {"dp": line, "tensor": tensor}, offset - 1
                ).start()
        for offset in range(n_dp):
            _, base = line_of(offset)
            for kind, buffer, sems in sets:
                if offset:
                    forward(kind, buffer, sems, base + tensor, to_x, 3 + offset).wait_recv()
                forward(kind, buffer, sems, base + tensor, to_x, 3 + offset).start()
                forward(kind, buffer, sems, base + tensor, to_core, 7 + offset).start()
        for offset in range(n_dp):
            _, base = line_of(offset)
            for kind, buffer, sems in sets:
                forward(kind, buffer, sems, base + x_peer, to_core, 11 + offset).wait_recv()
                forward(kind, buffer, sems, base + x_peer, to_core, 11 + offset).start()

    def gathered(sets):
        for offset in range(n_dp):
            base = lax.rem(dp + offset, n_dp) * n_tensor
            for kind, buffer, sems in sets:
                forward(kind, buffer, sems, base + core_peer, to_core, 7 + offset).wait_recv()
                far = lax.rem(core_peer + 2, 4)
                forward(kind, buffer, sems, base + far, to_core, 11 + offset).wait_recv()

    def drained(sets):
        for index in range(15):
            for kind, buffer, sems in sets:
                forward(kind, buffer, sems, me, to_core, index).wait_send()

    first = ((0, meta_all, meta_sem), (1, q_all, q_sem))
    spread_out(first)

    scale = 1.0 / math.sqrt(q_ref.shape[-1])
    fresh_rows = [
        new_ref[row, token, 0].astype(jnp.float32)
        for row in range(rows)
        for token in range(steps + 1)
    ]
    blank = jnp.zeros((16 - len(fresh_rows), 128), jnp.float32)
    fresh_k = jnp.concatenate([pair[0:1] for pair in fresh_rows] + [blank], axis=0)
    fresh_v = jnp.concatenate([pair[1:2] for pair in fresh_rows] + [blank], axis=0)
    fresh_k = fresh_k.astype(jnp.bfloat16)
    fresh_v = fresh_v.astype(jnp.bfloat16)
    resid_rows = [resid_ref[row].astype(jnp.float32) for row in range(rows)]
    resid = jnp.concatenate(
        [
            resid_rows[row][step : step + 1, head * 128 : (head + 1) * 128]
            for row in range(rows)
            for step in range(steps)
            for head in range(heads)
        ],
        axis=0,
    )
    fresh_scores = (
        lax.dot_general(
            q_ref[...],
            fresh_k,
            (((1,), (1,)), ((), ())),
            preferred_element_type=jnp.float32,
        )
        * scale
    )
    qi = lax.broadcasted_iota(jnp.int32, fresh_scores.shape, 0)
    fi = lax.broadcasted_iota(jnp.int32, fresh_scores.shape, 1)
    fresh = steps + 1
    fresh_ok = (fi // fresh == qi // (steps * heads)) & (
        fi % fresh <= (qi // heads) % steps + 1
    )
    fresh_scores = jnp.where(fresh_ok, fresh_scores, -1e30)
    fresh_top = jnp.max(fresh_scores, axis=1, keepdims=True)
    fresh_exp = jnp.where(fresh_ok, jnp.exp(fresh_scores - fresh_top), 0.0)
    fresh_total = jnp.sum(fresh_exp, axis=1, keepdims=True)
    fresh_out = jnp.dot(
        fresh_exp.astype(jnp.bfloat16), fresh_v, preferred_element_type=jnp.float32
    )

    def as_rows(first, second):
        lane = lax.broadcasted_iota(jnp.int32, (quer, 128), 1)
        both = jnp.where(lane == 0, first, jnp.where(lane == 1, second, 0.0))
        both = jnp.concatenate([both, jnp.zeros((128 - quer, 128), jnp.float32)], axis=0)
        return jnp.transpose(both)[0:8]

    fresh_rows = as_rows(fresh_top, fresh_total)

    gathered(first)

    ids = meta_all[:, 0, :]
    extra = meta_all[:, 1, :]
    local = ids - me * slots
    inside = (local >= 0) & (local < slots)
    row_i = lax.broadcasted_iota(jnp.int32, (pages, pages), 0)
    col_i = lax.broadcasted_iota(jnp.int32, (pages, pages), 1)
    before = jnp.where(row_i < col_i, 1.0, 0.0).astype(jnp.bfloat16)
    rank = jnp.dot(
        jnp.where(inside, 1.0, 0.0).astype(jnp.bfloat16), before, preferred_element_type=jnp.float32
    )
    capacity = max(2, (2 * pages + owners - 1) // owners)
    lane = lax.broadcasted_iota(jnp.int32, ids.shape, 1)
    slot_list = jnp.zeros(ids.shape, jnp.float32)
    code_list = jnp.zeros(ids.shape, jnp.float32)
    local_float = local.astype(jnp.float32)
    extra_float = extra.astype(jnp.float32)
    for k in range(capacity):
        chosen = inside & (rank == float(k))
        slot_k = jnp.sum(jnp.where(chosen, local_float, 0.0), axis=1, keepdims=True)
        code_k = jnp.sum(jnp.where(chosen, extra_float, 0.0), axis=1, keepdims=True)
        slot_list = jnp.where(lane == k, slot_k, slot_list)
        code_list = jnp.where(lane == k, code_k, code_list)
    list_vmem[...] = slot_list.astype(jnp.int32)
    list_copy = pltpu.make_async_copy(list_vmem, list_smem, list_sem)
    list_copy.start()
    keys = capacity * PAGE
    spread_k = lax.broadcasted_iota(jnp.int32, (pages, keys), 0)
    spread_c = lax.broadcasted_iota(jnp.int32, (pages, keys), 1)
    spread = jnp.where(spread_c // PAGE == spread_k, 1.0, 0.0).astype(jnp.bfloat16)
    code_ref[...] = jnp.dot(
        code_list.astype(jnp.bfloat16), spread, preferred_element_type=jnp.float32
    )
    list_copy.wait()
    pool_copy.wait()

    def attend(other, ready):
        code = code_ref[pl.ds(other, 1), :].astype(jnp.int32)
        key_rows = []
        value_rows = []
        for k in range(capacity):
            slot = jnp.clip(list_smem[other, k], 0, slots - 1)
            key_rows.append(pool[slot, 0])
            value_rows.append(pool[slot, 1])
        page_keys = jnp.concatenate(key_rows, axis=0)
        page_values = jnp.concatenate(value_rows, axis=0)
        scores = (
            lax.dot_general(
                q_all[other],
                page_keys,
                (((1,), (1,)), ((), ())),
                preferred_element_type=jnp.float32,
            )
            * scale
        )
        qi = lax.broadcasted_iota(jnp.int32, scores.shape, 0)
        ki = lax.broadcasted_iota(jnp.int32, scores.shape, 1)
        valid = (qi // heads == code // 32) & (ki % PAGE < code % 32)
        scores = jnp.where(valid, scores, -1e30)
        top = jnp.max(scores, axis=1, keepdims=True)
        weights = jnp.where(valid, jnp.exp(scores - top), 0.0)
        total = jnp.sum(weights, axis=1, keepdims=True)
        mixed = jnp.dot(
            weights.astype(jnp.bfloat16), page_values, preferred_element_type=jnp.float32
        )
        o_send[other] = mixed.astype(jnp.bfloat16)
        ml_send[other] = as_rows(top, total)

    def attend_peer(offset, carry):
        peer, device = peer_of(offset)
        attend(peer, None)
        remote(2, o_send.at[peer], o_all.at[me], o_sem, peer, device, me).start()
        remote(3, ml_send.at[peer], ml_all.at[me], ml_sem, peer, device, me).start()
        return carry

    lax.fori_loop(1, owners, attend_peer, 0)
    attend(me, None)
    o_all[me] = o_send[me]
    ml_all[me] = ml_send[me]

    def wait_parts(offset, carry):
        peer, device = peer_of(offset)
        remote(2, o_send.at[peer], o_all.at[peer], o_sem, peer, device, peer).wait_recv()
        remote(3, ml_send.at[peer], ml_all.at[peer], ml_sem, peer, device, peer).wait_recv()
        return carry

    lax.fori_loop(1, owners, wait_parts, 0)

    tops = ml_all[:, 0, :]
    totals = ml_all[:, 1, :]
    top = jnp.maximum(jnp.max(tops, axis=0, keepdims=True), fresh_rows[0:1])
    shares = jnp.exp(tops - top)
    fresh_share = jnp.exp(fresh_rows[0:1] - top)
    total = jnp.sum(shares * totals, axis=0, keepdims=True) + fresh_share * fresh_rows[1:2]
    total = jnp.where(lane[0:1] < quer, total, 1.0)
    shares = shares / total
    fresh_share = fresh_share / total
    every = jnp.concatenate(
        [shares, fresh_share, jnp.zeros((128 - owners - 1, 128), jnp.float32)], axis=0
    )
    columns = jnp.transpose(every)
    attn = fresh_out * columns[0:quer, owners : owners + 1]
    for owner in range(owners):
        attn = attn + o_all[owner].astype(jnp.float32) * columns[0:quer, owner : owner + 1]
    attended = (resid + attn).astype(jnp.bfloat16)
    x_all[me] = attended

    last = ((4, x_all, x_sem),)
    spread_out(last)
    rounded = attended.astype(jnp.float32)
    for row in range(rows):
        for head in range(heads):
            pair = [
                rounded[(row * steps + step) * heads + head :][0:1] for step in range(steps)
            ]
            att_ref[row, :, head * 128 : (head + 1) * 128] = jnp.concatenate(
                pair, axis=0
            ).astype(jnp.bfloat16)
    gathered(last)

    each = rows * steps
    tiles = depth // 128
    for line in range(n_dp):
        block = jnp.concatenate(
            [
                x_all[line * n_tensor + part].astype(jnp.float32).reshape(each, heads, 128)
                for part in range(n_tensor)
            ],
            axis=1,
        )
        squares = jnp.sum(jnp.sum(block * block, axis=1, keepdims=True), axis=2, keepdims=True)
        block = block * lax.rsqrt(squares / depth + 1e-05) * gain_ref[...][None]
        y_ref[line * each : (line + 1) * each] = block
    for tile in range(tiles):
        x_ref[:, tile * 128 : (tile + 1) * 128] = y_ref[:, tile, :].astype(jnp.bfloat16)

    def hidden_step(load, carry):
        slot = load
        for copy in gate_copies(load, slot):
            copy.wait()
        both = jnp.dot(x_ref[...], ring[slot], preferred_element_type=jnp.float32)
        gate_act = both[:, :128]
        value = gate_act / (1.0 + jnp.exp(-gate_act)) * both[:, 128:]
        h_ref[:, pl.ds(pl.multiple_of(load * 128, 128), 128)] = value.astype(jnp.bfloat16)

        @pl.when(load + ring_slots < loads)
        def _():
            for copy in down_copies(load + ring_slots - chunks, slot):
                copy.start()

        return carry

    lax.fori_loop(0, chunks, hidden_step, 0)

    pieces = 2
    per_piece = down_loads // pieces
    rows_piece = tiles // pieces

    core = lax.rem(tensor, 2)
    column = tensor // 2

    def piece_copy(piece, stage, source, target, device, index):
        return pltpu.make_async_remote_copy(
            src_ref=source,
            dst_ref=target,
            send_sem=p_send_sem.at[piece, stage, index],
            recv_sem=p_sem.at[piece, stage, index],
            device_id=device,
            device_id_type=pl.DeviceIdType.MESH,
        )

    def core_copy(piece):
        return piece_copy(piece, 0, core_send.at[piece], core_got.at[piece], to_core, 0)

    def x_copy(piece):
        return piece_copy(piece, 1, x_send.at[piece], x_got.at[piece], to_x, 0)

    def z_copy(piece, offset):
        line = lax.rem(dp + offset, n_dp)
        device = {"dp": line, "tensor": tensor}
        return piece_copy(
            piece,
            2,
            z_send.at[piece, offset],
            z_got.at[piece, offset],
            device,
            offset,
        )

    for piece in range(pieces):
        for step in range(per_piece):
            load = piece * per_piece + step
            slot = (chunks + load) % ring_slots
            for copy in down_copies(load, slot):
                copy.wait()
            for q in range(4):
                both = jnp.dot(
                    h_ref[...],
                    ring[slot, q * wide : (q + 1) * wide, :],
                    preferred_element_type=jnp.float32,
                )
                tile = load * 8 + 2 * q
                part_ref[:, tile, :] = both[:, :128]
                part_ref[:, tile + 1, :] = both[:, 128:]
        lines = slice(piece * rows_piece, (piece + 1) * rows_piece)
        for side in range(2):
            for line in range(n_dp):
                owner = line * n_tensor + side * 2 + 1 - core
                core_send[piece, side * n_dp + line] = part_ref[owner, lines].astype(jnp.bfloat16)
        core_copy(piece).start()

    for piece in range(pieces):
        lines = slice(piece * rows_piece, (piece + 1) * rows_piece)
        core_copy(piece).wait_recv()
        for line in range(n_dp):
            away = 1 - column
            far = part_ref[line * n_tensor + away * 2 + core, lines]
            far = far + core_got[piece, away * n_dp + line].astype(jnp.float32)
            x_send[piece, line] = far.astype(jnp.bfloat16)
        x_copy(piece).start()

    for piece in range(pieces):
        lines = slice(piece * rows_piece, (piece + 1) * rows_piece)
        x_copy(piece).wait_recv()
        for offset in range(n_dp):
            line = lax.rem(dp + offset, n_dp)
            near = part_ref[line * n_tensor + tensor, lines]
            near = near + core_got[piece, column * n_dp + line].astype(jnp.float32)
            near = near + x_got[piece, line].astype(jnp.float32)
            if offset:
                z_send[piece, offset] = near.astype(jnp.bfloat16)
                z_copy(piece, offset).start()
            else:
                part_ref[me, lines] = near

    for piece in range(pieces):
        lines = slice(piece * rows_piece, (piece + 1) * rows_piece)
        summed = part_ref[me, lines]
        for offset in range(1, n_dp):
            z_copy(piece, offset).wait_recv()
            summed = summed + z_got[piece, offset].astype(jnp.float32)
        for tile in range(rows_piece):
            at = (piece * rows_piece + tile) * 128
            out_ref[:, at : at + 128] = summed[tile : tile + 1].astype(jnp.bfloat16)

    drained(first)
    drained(last)
    for piece in range(pieces):
        core_copy(piece).wait_send()
        x_copy(piece).wait_send()
        for offset in range(1, n_dp):
            z_copy(piece, offset).wait_send()

    def drain(offset, carry):
        peer, device = peer_of(offset)
        remote(2, o_send.at[peer], o_all.at[me], o_sem, peer, device, me).wait_send()
        remote(3, ml_send.at[peer], ml_all.at[me], ml_sem, peer, device, me).wait_send()
        return carry

    lax.fori_loop(1, owners, drain, 0)


RING_SLOTS = 14


def fused_shards(
    resid,
    queries,
    new_kv,
    tail_fill,
    page_ids,
    kv_pool,
    norm_gain,
    gate_weight,
    up_weight,
    down_weight,
):
    n_dp = lax.axis_size("dp")
    n_tensor = lax.axis_size("tensor")
    owners = n_dp * n_tensor
    rows, steps, heads, head = queries.shape
    sel = page_ids.shape[-1]
    slots = kv_pool.shape[0]
    depth, wide = gate_weight.shape
    quer = rows * steps * heads
    tiles = depth // 128
    capacity = max(2, (2 * rows * steps * sel + owners - 1) // owners)
    dims = (n_dp, n_tensor, slots, wide, depth, RING_SLOTS, rows, steps, heads, sel)
    bf16, f32, i32 = jnp.bfloat16, jnp.float32, jnp.int32
    vmem = pl.BlockSpec(memory_space=pltpu.VMEM)
    hbm = pl.BlockSpec(memory_space=pl.ANY)
    dma = pltpu.SemaphoreType.DMA
    attended, ffn_out = pl.pallas_call(
        functools.partial(fused_kernel, dims),
        out_shape=(
            jax.ShapeDtypeStruct(resid.shape, bf16),
            jax.ShapeDtypeStruct((1, depth), bf16),
        ),
        in_specs=[vmem, vmem, pl.BlockSpec(memory_space=pltpu.SMEM)] + [vmem] * 3 + [hbm] * 4,
        out_specs=(vmem, vmem),
        scratch_shapes=[
            pltpu.VMEM((RING_SLOTS, depth, 256), bf16),
            pltpu.VMEM(kv_pool.shape, bf16),
            pltpu.VMEM((owners, 8, 128), i32),
            pltpu.VMEM((owners, quer, head), bf16),
            pltpu.VMEM((owners, quer, head), bf16),
            pltpu.VMEM((owners, quer, head), bf16),
            pltpu.VMEM((owners, 8, 128), f32),
            pltpu.VMEM((owners, 8, 128), f32),
            pltpu.VMEM((owners, quer, head), bf16),
            pltpu.VMEM((owners, 128), i32),
            pltpu.SMEM((owners, 128), i32),
            pltpu.VMEM((owners, capacity * PAGE), f32),
            pltpu.VMEM((owners, tiles, 128), f32),
            pltpu.VMEM((owners, depth), bf16),
            pltpu.VMEM((owners, wide), bf16),
            pltpu.VMEM((owners, tiles, 128), f32),
            pltpu.VMEM((2, 8, tiles // 2, 128), bf16),
            pltpu.VMEM((2, 8, tiles // 2, 128), bf16),
            pltpu.VMEM((2, n_dp, tiles // 2, 128), bf16),
            pltpu.VMEM((2, n_dp, tiles // 2, 128), bf16),
            pltpu.VMEM((2, n_dp, tiles // 2, 128), bf16),
            pltpu.VMEM((2, n_dp, tiles // 2, 128), bf16),
            dma(()),
            dma(()),
            dma((RING_SLOTS, 4)),
            dma((5, owners)),
            dma((owners,)),
            dma((owners,)),
            dma((owners,)),
            dma((owners,)),
            dma((owners,)),
            dma((2, 3, n_dp)),
            dma((2, 3, n_dp)),
        ],
        compiler_params=pltpu.CompilerParams(
            collective_id=0, has_side_effects=True, vmem_limit_bytes=VMEM_LIMIT
        ),
        name="attend_ffn",
    )(
        queries.reshape(quer, head),
        page_ids,
        tail_fill,
        new_kv,
        resid,
        norm_gain.reshape(tiles, 128),
        kv_pool,
        gate_weight,
        up_weight,
        down_weight,
    )
    return attended, ffn_out


VMEM_LIMIT = 65 * 1000 * 1000


def solution(mesh):
    in_specs = (
        P(("grp", "dp"), None, "tensor"),
        P(("grp", "dp"), None, "tensor", None),
        P(("grp", "dp"), None, "tensor", None, None),
        P(("grp", "dp"), None),
        P(("grp", "dp"), None, "tensor", None),
        P(("grp", "dp", "tensor"), None, None, None),
        P(),
        P(None, ("dp", "tensor")),
        P(None, ("dp", "tensor")),
        P(("dp", "tensor"), None),
    )
    out_specs = (P(("grp", "dp"), None, "tensor"), P(("grp", "dp", "tensor"), None))

    def whole(*arrays):
        fused = fits_fused(mesh, arrays[0], arrays[1], arrays[4], arrays[5], arrays[7])
        return jax.shard_map(
            fused_shards if fused else shards,
            mesh=mesh,
            in_specs=in_specs,
            out_specs=out_specs,
            check_vma=False,
        )(*arrays)

    return whole
```

```python
import functools
import math

import jax
import jax.numpy as jnp
from jax import lax
from jax.experimental import pallas as pl
from jax.experimental.pallas import tpu as pltpu
from jax.sharding import PartitionSpec as P

PAGE = 16
SEL = 32


def attend_group(query_group, page_keys, page_values, fresh_keys, fresh_values, fill_count):
    score_scale = 1.0 / math.sqrt(query_group.shape[-1])
    page_scores = (
        jnp.einsum("rshd,rskd->rshk", query_group, page_keys, preferred_element_type=jnp.float32)
        * score_scale
    )
    fresh_scores = (
        jnp.einsum("rshd,rjd->rshj", query_group, fresh_keys, preferred_element_type=jnp.float32)
        * score_scale
    )
    key_index = jnp.arange(page_keys.shape[2], dtype=jnp.int32)
    page_valid = (key_index[None, None, :] >= PAGE) | (
        key_index[None, None, :] < fill_count[:, :, None]
    )
    page_scores = jnp.where(page_valid[:, :, None, :], page_scores, -jnp.inf)
    fresh_index = jnp.arange(fresh_keys.shape[1], dtype=jnp.int32)
    step_index = jnp.arange(fill_count.shape[1], dtype=jnp.int32)
    fresh_valid = fresh_index[None, :] <= step_index[:, None] + 1
    fresh_scores = jnp.where(fresh_valid[None, :, None, :], fresh_scores, -jnp.inf)
    top_score = jnp.maximum(jnp.max(page_scores, axis=-1), jnp.max(fresh_scores, axis=-1))
    page_exp = jnp.exp(page_scores - top_score[..., None])
    fresh_exp = jnp.exp(fresh_scores - top_score[..., None])
    total = jnp.sum(page_exp, axis=-1) + jnp.sum(fresh_exp, axis=-1)
    page_weights = (page_exp / total[..., None]).astype(jnp.bfloat16)
    fresh_weights = (fresh_exp / total[..., None]).astype(jnp.bfloat16)
    page_part = jnp.einsum(
        "rshk,rskd->rshd", page_weights, page_values, preferred_element_type=jnp.float32
    )
    fresh_part = jnp.einsum(
        "rshj,rjd->rshd", fresh_weights, fresh_values, preferred_element_type=jnp.float32
    )
    return page_part + fresh_part


def shards(
    resid,
    queries,
    new_kv,
    tail_fill,
    page_ids,
    kv_pool,
    norm_gain,
    gate_weight,
    up_weight,
    down_weight,
):
    owner_total = lax.axis_size("dp") * lax.axis_size("tensor")
    pool_slots = kv_pool.shape[0]
    row_count = resid.shape[0]
    step_count = resid.shape[1]
    slot_list = page_ids.reshape(-1)
    request_total = slot_list.shape[0]
    capacity = max(2, (2 * request_total + owner_total - 1) // owner_total)
    owner_list = slot_list // pool_slots
    local_list = slot_list % pool_slots
    owner_onehot = (
        owner_list[:, None] == jnp.arange(owner_total, dtype=jnp.int32)[None, :]
    ).astype(jnp.int32)
    order_rank = jnp.sum(jnp.cumsum(owner_onehot, axis=0) * owner_onehot, axis=1) - 1
    position = owner_list * capacity + order_rank
    request_buffer = jnp.zeros((owner_total * capacity,), jnp.int32).at[position].set(local_list)
    request_buffer = request_buffer.reshape(owner_total, capacity)
    returned = lax.all_to_all(
        kv_pool[
            lax.all_to_all(
                request_buffer, ("dp", "tensor"), split_axis=0, concat_axis=0, tiled=True
            )
        ],
        ("dp", "tensor"),
        split_axis=0,
        concat_axis=0,
        tiled=True,
    )
    page_rows = returned.reshape((owner_total * capacity,) + kv_pool.shape[1:])[position]
    page_rows = page_rows.reshape(row_count, step_count, SEL, 2, PAGE, kv_pool.shape[-1])
    page_keys = page_rows[:, :, :, 0].reshape(row_count, step_count, SEL * PAGE, kv_pool.shape[-1])
    page_values = page_rows[:, :, :, 1].reshape(
        row_count, step_count, SEL * PAGE, kv_pool.shape[-1]
    )
    fresh_pair = new_kv[:, :, 0]
    attn = attend_group(
        queries, page_keys, page_values, fresh_pair[:, :, 0], fresh_pair[:, :, 1], tail_fill
    )
    attn = attn.reshape(row_count, step_count, resid.shape[2])
    attended = (resid.astype(jnp.float32) + attn).astype(jnp.bfloat16)
    full_rows = lax.all_gather(attended, "tensor", axis=2, tiled=True).astype(jnp.float32)
    mean_square = jnp.mean(full_rows * full_rows, axis=-1, keepdims=True)
    normed = (full_rows * lax.rsqrt(mean_square + 1e-05) * norm_gain).astype(jnp.bfloat16)
    block_rows = lax.all_gather(normed, "dp", axis=0, tiled=True)
    flat_rows = block_rows.reshape(-1, block_rows.shape[-1])
    gate_act = jnp.dot(flat_rows, gate_weight, preferred_element_type=jnp.float32)
    up_act = jnp.dot(flat_rows, up_weight, preferred_element_type=jnp.float32)
    hidden_rows = (jax.nn.silu(gate_act) * up_act).astype(jnp.bfloat16)
    hidden_all = hidden_rows.reshape(block_rows.shape[0], block_rows.shape[1], -1)
    hidden_flat = hidden_all.reshape(-1, hidden_all.shape[-1])
    summed = lax.psum_scatter(
        jnp.dot(hidden_flat, down_weight, preferred_element_type=jnp.float32),
        ("dp", "tensor"),
        scatter_dimension=0,
        tiled=True,
    )
    ffn_out = summed.astype(jnp.bfloat16)
    return (attended, ffn_out)


def fits_fused(mesh, resid, queries, page_ids, kv_pool, gate_weight):
    owners = mesh.shape["dp"] * mesh.shape["tensor"]
    rows = resid.shape[0] // (mesh.shape["grp"] * mesh.shape["dp"])
    steps = resid.shape[1]
    wide = gate_weight.shape[1] // owners
    return (
        owners == 16
        and mesh.shape["tensor"] == 4
        and rows * steps * mesh.shape["dp"] == owners
        and (queries.shape[2] // mesh.shape["tensor"]) % 8 == 0
        and rows * steps * (queries.shape[2] // mesh.shape["tensor"]) == 64
        and rows * steps * page_ids.shape[3] == 128
        and queries.shape[3] == 128
        and wide % 128 == 0
        and 4 * wide <= gate_weight.shape[0]
        and gate_weight.shape[0] % 1024 == 0
    )


def fused_kernel(
    dims,
    q_ref,
    ids_ref,
    fill_ref,
    new_ref,
    resid_ref,
    gain_ref,
    pool_hbm,
    gate_hbm,
    up_hbm,
    down_hbm,
    att_ref,
    out_ref,
    ring,
    pool,
    meta_all,
    q_all,
    o_send,
    o_all,
    ml_send,
    ml_all,
    x_all,
    list_vmem,
    list_smem,
    code_ref,
    y_ref,
    x_ref,
    h_ref,
    part_ref,
    core_send,
    core_got,
    x_send,
    x_got,
    z_send,
    z_got,
    pool_sem,
    list_sem,
    ring_sem,
    send_sem,
    meta_sem,
    q_sem,
    o_sem,
    ml_sem,
    x_sem,
    p_send_sem,
    p_sem,
):
    n_dp, n_tensor, slots, wide, depth, ring_slots, rows, steps, heads, sel = dims
    owners = n_dp * n_tensor
    dp = lax.axis_index("dp")
    tensor = lax.axis_index("tensor")
    me = dp * n_tensor + tensor
    chunks = wide // 128
    down_loads = depth // 1024
    loads = chunks + down_loads
    quer = rows * steps * heads
    pages = rows * steps * sel

    def gate_copies(load, slot):
        column = pl.multiple_of(load * 128, 128)
        return [
            pltpu.make_async_copy(
                source.at[:, pl.ds(column, 128)],
                ring.at[slot, :, pl.ds(128 * half, 128)],
                ring_sem.at[slot, half],
            )
            for half, source in ((0, gate_hbm), (1, up_hbm))
        ]

    def down_copies(load, slot):
        return [
            pltpu.make_async_copy(
                down_hbm.at[:, pl.ds(pl.multiple_of(load * 1024 + 256 * q, 256), 256)],
                ring.at[slot, pl.ds(q * wide, wide), :],
                ring_sem.at[slot, q],
            )
            for q in range(4)
        ]

    pool_copy = pltpu.make_async_copy(pool_hbm, pool, pool_sem)
    pool_copy.start()

    def peer_of(offset):
        peer = lax.rem(me + offset, owners)
        return peer, {"dp": peer // n_tensor, "tensor": peer % n_tensor}

    def remote(kind, source, target, sems, peer, device, index):
        return pltpu.make_async_remote_copy(
            src_ref=source,
            dst_ref=target,
            send_sem=send_sem.at[kind, peer],
            recv_sem=sems.at[index],
            device_id=device,
            device_id_type=pl.DeviceIdType.MESH,
        )

    barrier = pltpu.get_barrier_semaphore()

    def greet(offset, carry):
        _, device = peer_of(offset)
        pl.semaphore_signal(barrier, inc=1, device_id=device, device_id_type=pl.DeviceIdType.MESH)
        return carry

    lax.fori_loop(1, owners, greet, 0)

    def preload(load, carry):
        for copy in gate_copies(load, load):
            copy.start()
        return carry

    lax.fori_loop(0, min(chunks, ring_slots), preload, 0)
    for load in range(chunks, ring_slots):
        for copy in down_copies(load - chunks, load):
            copy.start()

    pl.semaphore_wait(barrier, owners - 1)

    page_lane = lax.broadcasted_iota(jnp.int32, (1, 128), 1)
    held = PAGE + 32 * (page_lane // sel)
    for row in range(rows):
        for step in range(steps):
            at = (row * steps + step) * sel
            meta_all[me, 0:1, at : at + sel] = ids_ref[row, step]
            held = jnp.where(page_lane == at, fill_ref[row, step] + 32 * (at // sel), held)
    meta_all[me, 1:2, :] = held
    q_all[me] = q_ref[...]

    core_peer = tensor + 1 - 2 * lax.rem(tensor, 2)
    x_peer = lax.rem(tensor + 2, 4)

    def forward(kind, buffer, sems, block, device, index):
        return pltpu.make_async_remote_copy(
            src_ref=buffer.at[block],
            dst_ref=buffer.at[block],
            send_sem=send_sem.at[kind, index],
            recv_sem=sems.at[block],
            device_id=device,
            device_id_type=pl.DeviceIdType.MESH,
        )

    to_core = {"dp": dp, "tensor": core_peer}
    to_x = {"dp": dp, "tensor": x_peer}

    def spread_out(sets):
        def line_of(offset):
            line = lax.rem(dp + offset, n_dp)
            return line, line * n_tensor

        for offset in range(1, n_dp):
            line, _ = line_of(offset)
            for kind, buffer, sems in sets:
                forward(
                    kind, buffer, sems, me, {"dp": line, "tensor": tensor}, offset - 1
                ).start()
        for offset in range(n_dp):
            _, base = line_of(offset)
            for kind, buffer, sems in sets:
                if offset:
                    forward(kind, buffer, sems, base + tensor, to_x, 3 + offset).wait_recv()
                forward(kind, buffer, sems, base + tensor, to_x, 3 + offset).start()
                forward(kind, buffer, sems, base + tensor, to_core, 7 + offset).start()
        for offset in range(n_dp):
            _, base = line_of(offset)
            for kind, buffer, sems in sets:
                forward(kind, buffer, sems, base + x_peer, to_core, 11 + offset).wait_recv()
                forward(kind, buffer, sems, base + x_peer, to_core, 11 + offset).start()

    def gathered(sets):
        for offset in range(n_dp):
            base = lax.rem(dp + offset, n_dp) * n_tensor
            for kind, buffer, sems in sets:
                forward(kind, buffer, sems, base + core_peer, to_core, 7 + offset).wait_recv()
                far = lax.rem(core_peer + 2, 4)
                forward(kind, buffer, sems, base + far, to_core, 11 + offset).wait_recv()

    def drained(sets):
        for index in range(15):
            for kind, buffer, sems in sets:
                forward(kind, buffer, sems, me, to_core, index).wait_send()

    first = ((0, meta_all, meta_sem), (1, q_all, q_sem))
    spread_out(first)

    scale = 1.0 / math.sqrt(q_ref.shape[-1])
    fresh_rows = [
        new_ref[row, token, 0].astype(jnp.float32)
        for row in range(rows)
        for token in range(steps + 1)
    ]
    blank = jnp.zeros((16 - len(fresh_rows), 128), jnp.float32)
    fresh_k = jnp.concatenate([pair[0:1] for pair in fresh_rows] + [blank], axis=0)
    fresh_v = jnp.concatenate([pair[1:2] for pair in fresh_rows] + [blank], axis=0)
    fresh_k = fresh_k.astype(jnp.bfloat16)
    fresh_v = fresh_v.astype(jnp.bfloat16)
    resid_rows = [resid_ref[row].astype(jnp.float32) for row in range(rows)]
    resid = jnp.concatenate(
        [
            resid_rows[row][step : step + 1, head * 128 : (head + 1) * 128]
            for row in range(rows)
            for step in range(steps)
            for head in range(heads)
        ],
        axis=0,
    )
    fresh_scores = (
        lax.dot_general(
            q_ref[...],
            fresh_k,
            (((1,), (1,)), ((), ())),
            preferred_element_type=jnp.float32,
        )
        * scale
    )
    qi = lax.broadcasted_iota(jnp.int32, fresh_scores.shape, 0)
    fi = lax.broadcasted_iota(jnp.int32, fresh_scores.shape, 1)
    fresh = steps + 1
    fresh_ok = (fi // fresh == qi // (steps * heads)) & (
        fi % fresh <= (qi // heads) % steps + 1
    )
    fresh_scores = jnp.where(fresh_ok, fresh_scores, -1e30)
    fresh_top = jnp.max(fresh_scores, axis=1, keepdims=True)
    fresh_exp = jnp.where(fresh_ok, jnp.exp(fresh_scores - fresh_top), 0.0)
    fresh_total = jnp.sum(fresh_exp, axis=1, keepdims=True)
    fresh_out = jnp.dot(
        fresh_exp.astype(jnp.bfloat16), fresh_v, preferred_element_type=jnp.float32
    )

    def as_rows(first, second):
        lane = lax.broadcasted_iota(jnp.int32, (quer, 128), 1)
        both = jnp.where(lane == 0, first, jnp.where(lane == 1, second, 0.0))
        both = jnp.concatenate([both, jnp.zeros((128 - quer, 128), jnp.float32)], axis=0)
        return jnp.transpose(both)[0:2]

    fresh_rows = as_rows(fresh_top, fresh_total)

    gathered(first)

    ids = meta_all[:, 0, :]
    extra = meta_all[:, 1, :]
    local = ids - me * slots
    inside = (local >= 0) & (local < slots)
    row_i = lax.broadcasted_iota(jnp.int32, (pages, pages), 0)
    col_i = lax.broadcasted_iota(jnp.int32, (pages, pages), 1)
    before = jnp.where(row_i < col_i, 1.0, 0.0).astype(jnp.bfloat16)
    rank = jnp.dot(
        jnp.where(inside, 1.0, 0.0).astype(jnp.bfloat16), before, preferred_element_type=jnp.float32
    )
    capacity = max(2, (2 * pages + owners - 1) // owners)
    lane = lax.broadcasted_iota(jnp.int32, ids.shape, 1)
    slot_list = jnp.zeros(ids.shape, jnp.float32)
    code_list = jnp.zeros(ids.shape, jnp.float32)
    local_float = local.astype(jnp.float32)
    extra_float = extra.astype(jnp.float32)
    for k in range(capacity):
        chosen = inside & (rank == float(k))
        slot_k = jnp.sum(jnp.where(chosen, local_float, 0.0), axis=1, keepdims=True)
        code_k = jnp.sum(jnp.where(chosen, extra_float, 0.0), axis=1, keepdims=True)
        slot_list = jnp.where(lane == k, slot_k, slot_list)
        code_list = jnp.where(lane == k, code_k, code_list)
    list_vmem[...] = slot_list.astype(jnp.int32)
    list_copy = pltpu.make_async_copy(list_vmem, list_smem, list_sem)
    list_copy.start()
    keys = capacity * PAGE
    spread_k = lax.broadcasted_iota(jnp.int32, (pages, keys), 0)
    spread_c = lax.broadcasted_iota(jnp.int32, (pages, keys), 1)
    spread = jnp.where(spread_c // PAGE == spread_k, 1.0, 0.0).astype(jnp.bfloat16)
    code_ref[...] = jnp.dot(
        code_list.astype(jnp.bfloat16), spread, preferred_element_type=jnp.float32
    )
    list_copy.wait()
    pool_copy.wait()

    def attend(other, ready):
        code = code_ref[pl.ds(other, 1), :].astype(jnp.int32)
        key_rows = []
        value_rows = []
        for k in range(capacity):
            slot = jnp.clip(list_smem[other, k], 0, slots - 1)
            key_rows.append(pool[slot, 0])
            value_rows.append(pool[slot, 1])
        page_keys = jnp.concatenate(key_rows, axis=0)
        page_values = jnp.concatenate(value_rows, axis=0)
        scores = (
            lax.dot_general(
                q_all[other],
                page_keys,
                (((1,), (1,)), ((), ())),
                preferred_element_type=jnp.float32,
            )
            * scale
        )
        qi = lax.broadcasted_iota(jnp.int32, scores.shape, 0)
        ki = lax.broadcasted_iota(jnp.int32, scores.shape, 1)
        valid = (qi // heads == code // 32) & (ki % PAGE < code % 32)
        scores = jnp.where(valid, scores, -1e30)
        top = jnp.max(scores, axis=1, keepdims=True)
        weights = jnp.where(valid, jnp.exp(scores - top), 0.0)
        total = jnp.sum(weights, axis=1, keepdims=True)
        mixed = jnp.dot(
            weights.astype(jnp.bfloat16), page_values, preferred_element_type=jnp.float32
        )
        o_send[other] = mixed.astype(jnp.bfloat16)
        ml_send[other] = as_rows(top, total)

    def attend_peer(offset, carry):
        peer, device = peer_of(offset)
        attend(peer, None)
        remote(2, o_send.at[peer], o_all.at[me], o_sem, peer, device, me).start()
        remote(3, ml_send.at[peer], ml_all.at[me], ml_sem, peer, device, me).start()
        return carry

    lax.fori_loop(1, owners, attend_peer, 0)
    attend(me, None)
    o_all[me] = o_send[me]
    ml_all[me] = ml_send[me]

    def wait_parts(offset, carry):
        peer, device = peer_of(offset)
        remote(2, o_send.at[peer], o_all.at[peer], o_sem, peer, device, peer).wait_recv()
        remote(3, ml_send.at[peer], ml_all.at[peer], ml_sem, peer, device, peer).wait_recv()
        return carry

    lax.fori_loop(1, owners, wait_parts, 0)

    tops = ml_all[:, 0, :]
    totals = ml_all[:, 1, :]
    top = jnp.maximum(jnp.max(tops, axis=0, keepdims=True), fresh_rows[0:1])
    shares = jnp.exp(tops - top)
    fresh_share = jnp.exp(fresh_rows[0:1] - top)
    total = jnp.sum(shares * totals, axis=0, keepdims=True) + fresh_share * fresh_rows[1:2]
    total = jnp.where(lane[0:1] < quer, total, 1.0)
    shares = shares / total
    fresh_share = fresh_share / total
    every = jnp.concatenate(
        [shares, fresh_share, jnp.zeros((128 - owners - 1, 128), jnp.float32)], axis=0
    )
    columns = jnp.transpose(every)
    attn = fresh_out * columns[0:quer, owners : owners + 1]
    for owner in range(owners):
        attn = attn + o_all[owner].astype(jnp.float32) * columns[0:quer, owner : owner + 1]
    attended = (resid + attn).astype(jnp.bfloat16)
    x_all[me] = attended

    last = ((4, x_all, x_sem),)
    spread_out(last)
    rounded = attended.astype(jnp.float32)
    for row in range(rows):
        for head in range(heads):
            pair = [
                rounded[(row * steps + step) * heads + head :][0:1] for step in range(steps)
            ]
            att_ref[row, :, head * 128 : (head + 1) * 128] = jnp.concatenate(
                pair, axis=0
            ).astype(jnp.bfloat16)
    gathered(last)

    each = rows * steps
    tiles = depth // 128
    for line in range(n_dp):
        block = jnp.concatenate(
            [
                x_all[line * n_tensor + part].astype(jnp.float32).reshape(each, heads, 128)
                for part in range(n_tensor)
            ],
            axis=1,
        )
        squares = jnp.sum(jnp.sum(block * block, axis=1, keepdims=True), axis=2, keepdims=True)
        block = block * lax.rsqrt(squares / depth + 1e-05) * gain_ref[...][None]
        y_ref[line * each : (line + 1) * each] = block
    for tile in range(tiles):
        x_ref[:, tile * 128 : (tile + 1) * 128] = y_ref[:, tile, :].astype(jnp.bfloat16)

    def hidden_step(load, carry):
        slot = load
        for copy in gate_copies(load, slot):
            copy.wait()
        both = jnp.dot(x_ref[...], ring[slot], preferred_element_type=jnp.float32)
        gate_act = both[:, :128]
        value = gate_act / (1.0 + jnp.exp(-gate_act)) * both[:, 128:]
        h_ref[:, pl.ds(pl.multiple_of(load * 128, 128), 128)] = value.astype(jnp.bfloat16)

        @pl.when(load + ring_slots < loads)
        def _():
            for copy in down_copies(load + ring_slots - chunks, slot):
                copy.start()

        return carry

    lax.fori_loop(0, chunks, hidden_step, 0)

    pieces = 2
    per_piece = down_loads // pieces
    rows_piece = tiles // pieces

    core = lax.rem(tensor, 2)
    column = tensor // 2

    def piece_copy(piece, stage, source, target, device, index):
        return pltpu.make_async_remote_copy(
            src_ref=source,
            dst_ref=target,
            send_sem=p_send_sem.at[piece, stage, index],
            recv_sem=p_sem.at[piece, stage, index],
            device_id=device,
            device_id_type=pl.DeviceIdType.MESH,
        )

    def core_copy(piece):
        return piece_copy(piece, 0, core_send.at[piece], core_got.at[piece], to_core, 0)

    def x_copy(piece):
        return piece_copy(piece, 1, x_send.at[piece], x_got.at[piece], to_x, 0)

    def z_copy(piece, offset):
        line = lax.rem(dp + offset, n_dp)
        device = {"dp": line, "tensor": tensor}
        return piece_copy(
            piece,
            2,
            z_send.at[piece, offset],
            z_got.at[piece, offset],
            device,
            offset,
        )

    for piece in range(pieces):
        for step in range(per_piece):
            load = piece * per_piece + step
            slot = (chunks + load) % ring_slots
            for copy in down_copies(load, slot):
                copy.wait()
            for q in range(4):
                both = jnp.dot(
                    h_ref[...],
                    ring[slot, q * wide : (q + 1) * wide, :],
                    preferred_element_type=jnp.float32,
                )
                tile = load * 8 + 2 * q
                part_ref[:, tile, :] = both[:, :128]
                part_ref[:, tile + 1, :] = both[:, 128:]
        lines = slice(piece * rows_piece, (piece + 1) * rows_piece)
        for side in range(2):
            for line in range(n_dp):
                owner = line * n_tensor + side * 2 + 1 - core
                core_send[piece, side * n_dp + line] = part_ref[owner, lines].astype(jnp.bfloat16)
        core_copy(piece).start()

    for piece in range(pieces):
        lines = slice(piece * rows_piece, (piece + 1) * rows_piece)
        core_copy(piece).wait_recv()
        for line in range(n_dp):
            away = 1 - column
            far = part_ref[line * n_tensor + away * 2 + core, lines]
            far = far + core_got[piece, away * n_dp + line].astype(jnp.float32)
            x_send[piece, line] = far.astype(jnp.bfloat16)
        x_copy(piece).start()

    for piece in range(pieces):
        lines = slice(piece * rows_piece, (piece + 1) * rows_piece)
        x_copy(piece).wait_recv()
        for offset in range(n_dp):
            line = lax.rem(dp + offset, n_dp)
            near = part_ref[line * n_tensor + tensor, lines]
            near = near + core_got[piece, column * n_dp + line].astype(jnp.float32)
            near = near + x_got[piece, line].astype(jnp.float32)
            if offset:
                z_send[piece, offset] = near.astype(jnp.bfloat16)
                z_copy(piece, offset).start()
            else:
                part_ref[me, lines] = near

    for piece in range(pieces):
        lines = slice(piece * rows_piece, (piece + 1) * rows_piece)
        summed = part_ref[me, lines]
        for offset in range(1, n_dp):
            z_copy(piece, offset).wait_recv()
            summed = summed + z_got[piece, offset].astype(jnp.float32)
        for tile in range(rows_piece):
            at = (piece * rows_piece + tile) * 128
            out_ref[:, at : at + 128] = summed[tile : tile + 1].astype(jnp.bfloat16)

    drained(first)
    drained(last)
    for piece in range(pieces):
        core_copy(piece).wait_send()
        x_copy(piece).wait_send()
        for offset in range(1, n_dp):
            z_copy(piece, offset).wait_send()

    def drain(offset, carry):
        peer, device = peer_of(offset)
        remote(2, o_send.at[peer], o_all.at[me], o_sem, peer, device, me).wait_send()
        remote(3, ml_send.at[peer], ml_all.at[me], ml_sem, peer, device, me).wait_send()
        return carry

    lax.fori_loop(1, owners, drain, 0)


RING_SLOTS = 14


def fused_shards(
    resid,
    queries,
    new_kv,
    tail_fill,
    page_ids,
    kv_pool,
    norm_gain,
    gate_weight,
    up_weight,
    down_weight,
):
    n_dp = lax.axis_size("dp")
    n_tensor = lax.axis_size("tensor")
    owners = n_dp * n_tensor
    rows, steps, heads, head = queries.shape
    sel = page_ids.shape[-1]
    slots = kv_pool.shape[0]
    depth, wide = gate_weight.shape
    quer = rows * steps * heads
    tiles = depth // 128
    capacity = max(2, (2 * rows * steps * sel + owners - 1) // owners)
    dims = (n_dp, n_tensor, slots, wide, depth, RING_SLOTS, rows, steps, heads, sel)
    bf16, f32, i32 = jnp.bfloat16, jnp.float32, jnp.int32
    vmem = pl.BlockSpec(memory_space=pltpu.VMEM)
    hbm = pl.BlockSpec(memory_space=pl.ANY)
    dma = pltpu.SemaphoreType.DMA
    attended, ffn_out = pl.pallas_call(
        functools.partial(fused_kernel, dims),
        out_shape=(
            jax.ShapeDtypeStruct(resid.shape, bf16),
            jax.ShapeDtypeStruct((1, depth), bf16),
        ),
        in_specs=[vmem, vmem, pl.BlockSpec(memory_space=pltpu.SMEM)] + [vmem] * 3 + [hbm] * 4,
        out_specs=(vmem, vmem),
        scratch_shapes=[
            pltpu.VMEM((RING_SLOTS, depth, 256), bf16),
            pltpu.VMEM(kv_pool.shape, bf16),
            pltpu.VMEM((owners, 2, 128), i32),
            pltpu.VMEM((owners, quer, head), bf16),
            pltpu.VMEM((owners, quer, head), bf16),
            pltpu.VMEM((owners, quer, head), bf16),
            pltpu.VMEM((owners, 2, 128), f32),
            pltpu.VMEM((owners, 2, 128), f32),
            pltpu.VMEM((owners, quer, head), bf16),
            pltpu.VMEM((owners, 128), i32),
            pltpu.SMEM((owners, 128), i32),
            pltpu.VMEM((owners, capacity * PAGE), f32),
            pltpu.VMEM((owners, tiles, 128), f32),
            pltpu.VMEM((owners, depth), bf16),
            pltpu.VMEM((owners, wide), bf16),
            pltpu.VMEM((owners, tiles, 128), f32),
            pltpu.VMEM((2, 8, tiles // 2, 128), bf16),
            pltpu.VMEM((2, 8, tiles // 2, 128), bf16),
            pltpu.VMEM((2, n_dp, tiles // 2, 128), bf16),
            pltpu.VMEM((2, n_dp, tiles // 2, 128), bf16),
            pltpu.VMEM((2, n_dp, tiles // 2, 128), bf16),
            pltpu.VMEM((2, n_dp, tiles // 2, 128), bf16),
            dma(()),
            dma(()),
            dma((RING_SLOTS, 4)),
            dma((5, owners)),
            dma((owners,)),
            dma((owners,)),
            dma((owners,)),
            dma((owners,)),
            dma((owners,)),
            dma((2, 3, n_dp)),
            dma((2, 3, n_dp)),
        ],
        compiler_params=pltpu.CompilerParams(
            collective_id=0, has_side_effects=True, vmem_limit_bytes=VMEM_LIMIT
        ),
        name="attend_ffn",
    )(
        queries.reshape(quer, head),
        page_ids,
        tail_fill,
        new_kv,
        resid,
        norm_gain.reshape(tiles, 128),
        kv_pool,
        gate_weight,
        up_weight,
        down_weight,
    )
    return attended, ffn_out


VMEM_LIMIT = 65 * 1000 * 1000


def solution(mesh):
    in_specs = (
        P(("grp", "dp"), None, "tensor"),
        P(("grp", "dp"), None, "tensor", None),
        P(("grp", "dp"), None, "tensor", None, None),
        P(("grp", "dp"), None),
        P(("grp", "dp"), None, "tensor", None),
        P(("grp", "dp", "tensor"), None, None, None),
        P(),
        P(None, ("dp", "tensor")),
        P(None, ("dp", "tensor")),
        P(("dp", "tensor"), None),
    )
    out_specs = (P(("grp", "dp"), None, "tensor"), P(("grp", "dp", "tensor"), None))

    def whole(*arrays):
        fused = fits_fused(mesh, arrays[0], arrays[1], arrays[4], arrays[5], arrays[7])
        return jax.shard_map(
            fused_shards if fused else shards,
            mesh=mesh,
            in_specs=in_specs,
            out_specs=out_specs,
            check_vma=False,
        )(*arrays)

    return whole
```
